32 devices in a mesh: ab: 16 (over z, y, x), cd: 2 (over core).
Axes of the slice: x: 2, y: 2, z: 4, core: 2. Of those that a mesh axis runs over, the one named last changes fastest.
Arguments:
- amplitudes: bfloat16 [48, 16, 3072], P('ab', None, 'cd'), may hold values from -6 to 6
- integral: bfloat16 [49152, 20480], P('ab', 'cd'), may hold values from -0.02734375 to 0.02734375
Outputs:
- ladder: float32 [48, 20480], P('ab', 'cd')
The draws below stay inside these ranges and needn't reach their ends.
All inputs are finite; a program needn't handle non-finite values.
Results may differ from the reference program's by a relative error of at most 0.0003.
Values may be sent and summed in bfloat16 or wider, within the bound.
No kernel may reach another device: no remote copies, remote signals or barrier semaphores. Data moves between devices by JAX's collectives and lax.ppermute only.
A program may use at most 128 MiB of HBM per device.

```python
import jax
import jax.numpy as jnp
from jax import lax

CD = 49152
AB = 20480
PAIRS = 48
BLOCK = 3072
N_CD = 2


def raised(array, own_key, source, target, blocks, factor):
    owner, partner = [(jnp.arange(array.shape[dim]) // (array.shape[dim] // blocks)).reshape([-1 if axis == dim else 1 for axis in range(array.ndim)]) for dim in (source, target)]
    chosen = jax.random.permutation(own_key, blocks)[partner]
    strong = (owner == chosen) | (owner == (partner + blocks // 2) % blocks)
    return jnp.where(strong, factor * array, array)


def level_of(stream_key, shape, pieces, low, largest):
    factor_of, own = 1.0, jax.random.fold_in(stream_key, 6)
    for axis_at, blocks in pieces:
        heights = jnp.exp(jax.random.uniform(jax.random.fold_in(own, axis_at), (blocks,), jnp.float32, low / len(pieces), largest / len(pieces)))
        factor_of = factor_of * jnp.repeat(heights, shape[axis_at] // blocks).reshape([-1 if axis == axis_at else 1 for axis in range(len(shape))])
    return factor_of


def gaussian(stream_key, extent, scale, reach, shards=(), kind=jnp.bfloat16):
    entries = jax.random.normal(stream_key, extent, jnp.float32) * scale
    if len(shards) > 0:
        entries = level_of(stream_key, extent, shards, -0.22, 0.18) * entries
    return jnp.clip(entries, min=-reach, max=reach).astype(kind)


def bell_draw_with(rng, dims, scale, reach, cuts, heavy, kind=jnp.bfloat16):
    entries = scale * jax.random.normal(rng, dims, jnp.float32)
    if cuts:
        entries = entries * level_of(rng, dims, cuts, -0.22, 0.18)
    return jnp.clip(raised(entries, jax.random.fold_in(rng, 3), *heavy), -reach, reach).astype(kind)


def setup_inputs(seed: int = 0) -> dict:
    key_of = jax.random.split(jax.random.key(seed), 3)
    return {
        "amplitudes": bell_draw_with(key_of[0], (PAIRS, CD // BLOCK, BLOCK), 1.0, 6.0, ((0, 16), (2, 2)), (1, 0, 16, 2.0)),
        "integral": gaussian(key_of[1], (CD, AB), CD ** -0.5, 0.02734375, ((0, 16), (1, 2))),
    }


def reference(amplitudes, integral):
    t2_matrix = amplitudes.reshape(PAIRS, CD).astype(jnp.float32)
    width = AB // N_CD

    def one_block(index):
        start = (index * width).astype(jnp.int32)
        columns = lax.dynamic_slice_in_dim(integral, start, width, 1).astype(jnp.float32)
        return jnp.dot(t2_matrix, columns, precision=lax.Precision.HIGHEST)

    blocks = lax.map(one_block, jnp.arange(N_CD, dtype=jnp.int32))
    return jnp.transpose(blocks, (1, 0, 2)).reshape(PAIRS, AB)
```

```python
import functools
import math

import jax
import jax.numpy as jnp
from jax import lax
from jax.experimental import pallas as pl
from jax.experimental.pallas import tpu as pltpu
from jax.sharding import PartitionSpec as P

F32, BF16 = jnp.float32, jnp.bfloat16
PLANE = 4
UNITS = 20
AHEAD = (2, 5)
STREAM = 7
SECOND = 6
MORE = 2
SLOTS = 4
PIECES = 4
TILE = 512
MATRIX = 256
LANES = 128
TOP, TINY = 1440.0, 1e-30
SMALL = pl.CostEstimate(flops=1 << 20, bytes_accessed=1 << 20, transcendentals=0)
VMEM = 14 << 20


def select(rows, columns, source):
    row = lax.broadcasted_iota(jnp.int32, (rows, columns), 0)
    column = lax.broadcasted_iota(jnp.int32, (rows, columns), 1)
    return (column == source(row)).astype(BF16)


def copies(integral, start, unit, target, sems):
    step = target.shape[0] // PIECES
    return [
        pltpu.make_async_copy(
            integral.at[pl.ds(i * step, step), pl.ds(start, unit)],
            target.at[pl.ds(i * step, step), :],
            sems.at[i],
        )
        for i in range(PIECES)
    ]


def load(start, columns, unit, integral, after):
    depth = integral.shape[0]

    def kernel(integral_ref, after_ref, out_ref, sems):
        moves = []
        for k in range(columns // unit):
            target = out_ref.at[:, pl.ds(k * unit, unit)]
            moves += copies(integral_ref, start + k * unit, unit, target, sems.at[k])
        for move in moves:
            move.start()
        for move in moves:
            move.wait()

    return pl.pallas_call(
        kernel,
        out_shape=pltpu.VMEM((depth, columns), BF16),
        in_specs=[pl.BlockSpec(memory_space=pl.ANY)] * 2,
        out_specs=pl.BlockSpec(memory_space=pltpu.VMEM),
        scratch_shapes=[pltpu.SemaphoreType.DMA((columns // unit, PIECES))],
        compiler_params=pltpu.CompilerParams(vmem_limit_bytes=VMEM),
        cost_estimate=pl.CostEstimate(flops=0, bytes_accessed=depth * columns * 2, transcendentals=0),
    )(integral, after)


def encode(sums, largest):
    scale = (TOP / jnp.maximum(largest, TINY)).astype(BF16)
    scaled = sums * scale.astype(F32)
    square = scaled * scaled
    fourth = square * square
    return (fourth * fourth * square * (scaled * jnp.abs(scaled))).astype(BF16), scale


def decode(code, scale):
    code = code.astype(F32)
    size = jnp.exp2(jnp.log2(jnp.abs(code)) * (1.0 / 12.0)) * (1.0 / scale.astype(F32))
    return jnp.where(code < 0, -size, size)


def fold(group):
    return 8 // math.gcd(group, 8)


def packed_rows(group, part):
    whole = group // 8 * 8
    rest = group - whole
    rows = [(0, whole, part * whole)] if whole else []
    return rows + ([(whole, rest, fold(group) * whole + part * rest)] if rest else [])


def unpacked(array, group, start, count):
    parts = fold(group)
    whole = group // 8 * 8
    rest = group - whole
    out = []
    for j in range(parts):
        pieces = []
        if start < whole:
            pieces.append(array[j * whole + start : j * whole + min(start + count, whole)])
        if start + count > whole:
            at = parts * whole + j * rest - whole
            pieces.append(array[at + max(start, whole) : at + start + count])
        out.append(pieces[0] if len(pieces) == 1 else jnp.concatenate(pieces, axis=0))
    return out


def split_by_plane(halves, lines):
    pairs, blocks, offsets = halves[0].shape
    cores, group = len(halves), lines * pairs
    rows = cores * group

    def kernel(*refs):
        me, core = lax.axis_index("ab"), lax.axis_index("cd")
        total = 0.0
        for j, ref in enumerate(refs[:cores]):

            def source(row):
                r, h, s, p = row // rows, row % rows // group, row % group // pairs, row % pairs
                column = p * blocks + jnp.bitwise_xor(s * PLANE + r, me)
                return jnp.where(h == jnp.bitwise_xor(core, j), column, -1)

            flat = ref[...].reshape(pairs * blocks, offsets)
            total += jnp.dot(select(PLANE * rows, pairs * blocks, source), flat, preferred_element_type=F32)
        for r, out in enumerate(refs[cores:]):
            out[...] = total[r * rows : (r + 1) * rows].astype(BF16)

    shape = jax.ShapeDtypeStruct((rows, offsets), BF16)
    return pl.pallas_call(
        kernel,
        out_shape=[shape] * PLANE,
        in_specs=[pl.BlockSpec(memory_space=pltpu.VMEM)] * cores,
        out_specs=[pl.BlockSpec(memory_space=pltpu.VMEM)] * PLANE,
        compiler_params=pltpu.CompilerParams(vmem_limit_bytes=VMEM),
        cost_estimate=SMALL,
    )(*halves)


def split_by_line(parts, cores, lines, pairs, after):
    offsets = parts[0].shape[1]
    group, rows = lines * pairs, cores * PLANE * pairs

    def kernel(*refs):
        total = 0.0
        for r, ref in enumerate(refs[:PLANE]):

            def source(row):
                s, h, at, p = row // rows, row % rows // (PLANE * pairs), row % rows // pairs % PLANE, row % pairs
                return jnp.where(at == r, h * group + s * pairs + p, -1)

            total += jnp.dot(select(lines * rows, cores * group, source), ref[...], preferred_element_type=F32)
        for s, out in enumerate(refs[PLANE + 1 :]):
            out[...] = total[s * rows : (s + 1) * rows].astype(BF16)

    shape = jax.ShapeDtypeStruct((rows, offsets), BF16)
    return pl.pallas_call(
        kernel,
        out_shape=[shape] * lines,
        in_specs=[pl.BlockSpec(memory_space=pltpu.VMEM)] * PLANE + [pl.BlockSpec(memory_space=pl.ANY)],
        out_specs=[pl.BlockSpec(memory_space=pltpu.VMEM)] * lines,
        compiler_params=pltpu.CompilerParams(vmem_limit_bytes=VMEM),
        cost_estimate=SMALL,
    )(*parts, after)


def gather_window(parts, cores, pairs, after):
    lines = len(parts)
    rows, offsets = parts[0].shape
    group = lines * pairs
    taken = PLANE * group

    def kernel(*refs):
        total = 0.0
        for s in range(lines):

            def source(row):
                h, r, at, p = row // taken, row % taken // group, row % group // pairs, row % pairs
                return jnp.where(at == s, (h * PLANE + r) * pairs + p, -1)

            total += jnp.dot(select(cores * taken, rows, source), refs[s][...], preferred_element_type=F32)
        for h in range(cores):
            refs[-1][:, pl.ds(h * offsets, offsets)] = total[h * taken : (h + 1) * taken].astype(BF16)

    return pl.pallas_call(
        kernel,
        out_shape=jax.ShapeDtypeStruct((taken, cores * offsets), BF16),
        in_specs=[pl.BlockSpec(memory_space=pltpu.VMEM)] * lines + [pl.BlockSpec(memory_space=pl.ANY)],
        out_specs=pl.BlockSpec(memory_space=pltpu.VMEM),
        compiler_params=pltpu.CompilerParams(vmem_limit_bytes=VMEM),
        cost_estimate=SMALL,
    )(*parts, after)


def multiply(window_ref, chunk_ref, at, tile):
    rows, depth = window_ref.shape
    half = tile // 2
    if half != MATRIX or depth % MATRIX or rows % 16:
        return jnp.dot(window_ref[...], chunk_ref[:, pl.ds(at, tile)], preferred_element_type=F32)

    def body(*sums):
        for k in range(depth // MATRIX):
            ks = pl.ds(k * MATRIX, MATRIX)
            for unit in range(2):
                pltpu.matmul_push_rhs(chunk_ref[ks, pl.ds(at + unit * half, half)], k % 2, unit)
            for unit in range(2):
                pltpu.matmul_acc_lhs(sums[unit], window_ref[:, ks], k % 2)
        return jnp.concatenate([pltpu.matmul_pop(sums[unit]) for unit in range(2)], axis=1)

    return pl.run_scoped(body, pltpu.ACC(0)((rows, half), F32), pltpu.ACC(1)((rows, half), F32))


def product(window, integral, ready, start, stream, more, unit, after):
    group = window.shape[0] // PLANE
    depth = integral.shape[0]
    parts = fold(group)
    columns = sum(chunk.shape[1] for chunk in ready) + stream
    width = columns // parts
    tile = next(t for t in (TILE, 256, 128) if unit % t == 0)
    steps = stream // unit

    def kernel(window_ref, integral_ref, *refs):
        chunks, refs = refs[: len(ready)], refs[len(ready) + len(after) :]
        own, outs, refs = refs[0], refs[1:PLANE], refs[PLANE:]
        kept, ring, sems, more_sems = refs[-4:]
        incoming = [
            copies(integral_ref, start + k * unit, unit, ring.at[k % SLOTS], sems.at[k % SLOTS]) for k in range(steps)
        ]
        handed = [
            copies(integral_ref, start + stream + k * unit, unit, refs[0].at[:, pl.ds(k * unit, unit)], more_sems.at[k])
            for k in range(more // unit)
        ]
        for move in sum(incoming[: SLOTS - 1], []):
            move.start()

        def tiles(chunk_ref, column, largest):
            part, offset = divmod(column, width)

            def step(i, largest):
                at = pl.multiple_of(i * tile, tile)
                sums = multiply(window_ref, chunk_ref, at, tile)
                at = pl.ds(offset + at, tile)
                for begin, rows, where in packed_rows(group, part):
                    own[where : where + rows, at] = sums[begin : begin + rows]
                    for r in range(1, PLANE):
                        kept[r - 1, where : where + rows, at] = sums[r * group + begin : r * group + begin + rows]
                return jnp.maximum(largest, jnp.abs(sums[group:]))

            return lax.fori_loop(0, unit // tile, step, largest)

        held = [
            chunk_ref.at[:, pl.ds(at, unit)] for chunk_ref in chunks for at in range(0, chunk_ref.shape[1], unit)
        ]
        largest = jnp.zeros(((PLANE - 1) * group, tile), F32)
        for k in range(max(len(held), steps)):
            if k < len(held):
                largest = tiles(held[k], k * unit, largest)
            if k < steps:
                for move in incoming[k]:
                    move.wait()
                for move in incoming[k + SLOTS - 1] if k + SLOTS - 1 < steps else []:
                    move.start()
                largest = tiles(ring.at[k % SLOTS], (len(held) + k) * unit, largest)
            if k % 3 == 2 and k // 3 < len(handed):
                for move in handed[k // 3]:
                    move.start()

        largest = jnp.max(largest, keepdims=True)
        for r, out in enumerate(outs):

            @pl.loop(0, width // tile)
            def _(i):
                at = pl.ds(pl.multiple_of(i * tile, tile), tile)
                out[:, at] = encode(kept[r, :, at], largest)[0]

            out[:, pl.ds(width, LANES)] = jnp.broadcast_to(encode(largest, largest)[1], (parts * group, LANES))
        for move in sum(handed, []):
            move.wait()

    shapes = [pltpu.VMEM((parts * group, width), F32)]
    shapes += [pltpu.VMEM((parts * group, width + LANES), BF16)] * (PLANE - 1)
    if more:
        shapes.append(pltpu.VMEM((depth, more), BF16))
    ready = [pltpu.with_memory_space_constraint(chunk, pltpu.VMEM) for chunk in ready]
    return pl.pallas_call(
        kernel,
        out_shape=shapes,
        in_specs=[pl.BlockSpec(memory_space=pltpu.VMEM), pl.BlockSpec(memory_space=pl.ANY)]
        + [pl.BlockSpec(memory_space=pltpu.VMEM)] * len(ready)
        + [pl.BlockSpec(memory_space=pl.ANY)] * len(after),
        out_specs=[pl.BlockSpec(memory_space=pltpu.VMEM)] * len(shapes),
        scratch_shapes=[
            pltpu.VMEM((PLANE - 1, parts * group, width), F32),
            pltpu.VMEM((min(SLOTS, steps), depth, unit), BF16),
            pltpu.SemaphoreType.DMA((min(SLOTS, steps), PIECES)),
            pltpu.SemaphoreType.DMA((max(more // unit, 1), PIECES)),
        ],
        compiler_params=pltpu.CompilerParams(vmem_limit_bytes=VMEM),
        cost_estimate=pl.CostEstimate(
            flops=2 * window.shape[0] * depth * columns, bytes_accessed=depth * columns * 2, transcendentals=0
        ),
    )(window, integral, *ready, *after)


def line_fold(width, parts):
    return next(n for n in (8, 4, 2, 1) if n * parts <= 8 and width % (n * LANES) == 0)


def add_plane(chunk, lines, pairs):
    group = lines * pairs
    parts = fold(group)
    width = chunk[0].shape[1]
    pieces = line_fold(width, parts)
    rows, columns = parts * pieces * pairs, width // pieces

    def kernel(*refs):
        ins, own, outs, kept = refs[:PLANE], refs[PLANE], refs[PLANE + 1 : -1], refs[-1]
        total = ins[0][...]
        for ref in ins[1:]:
            total += decode(ref[:, pl.ds(0, width)], ref[:, pl.ds(width, 1)])
        for s in range(lines):
            for j, part in enumerate(unpacked(total, group, s * pairs, pairs)):
                for k in range(pieces):
                    row = pl.ds((j * pieces + k) * pairs, pairs)
                    value = part[:, k * columns : (k + 1) * columns]
                    if s == 0:
                        own[row, :] = value
                    else:
                        kept[s - 1, row, :] = value
        largest = jnp.max(jnp.abs(total), keepdims=True)
        for s, out in enumerate(outs):
            code, scale = encode(kept[s], largest)
            out[:, pl.ds(0, columns)] = code
            out[:, pl.ds(columns, LANES)] = jnp.broadcast_to(scale, (rows, LANES))

    code = jax.ShapeDtypeStruct((rows, columns + LANES), BF16)
    return pl.pallas_call(
        kernel,
        out_shape=[jax.ShapeDtypeStruct((rows, columns), F32)] + [code] * (lines - 1),
        in_specs=[pl.BlockSpec(memory_space=pltpu.VMEM)] * PLANE,
        out_specs=[pl.BlockSpec(memory_space=pltpu.VMEM)] * lines,
        scratch_shapes=[pltpu.VMEM((lines - 1, rows, columns), F32)],
        compiler_params=pltpu.CompilerParams(vmem_limit_bytes=VMEM),
        cost_estimate=SMALL,
    )(*chunk)


def add_line(own, codes, before, pairs):
    columns = own.shape[1]

    def kernel(own_ref, *refs):
        out = refs[-1]
        total = own_ref[...]
        for ref in refs[: len(codes)]:
            total += decode(ref[:, pl.ds(0, columns)], ref[:, pl.ds(columns, 1)])
        if not before:
            out[...] = total
            return
        start = 0
        for array in [ref[...] for ref in refs[len(codes) : -1]] + [total]:
            for j in range(array.shape[0] // pairs):
                out[:, pl.ds(start, array.shape[1])] = array[j * pairs : (j + 1) * pairs]
                start += array.shape[1]

    size = sum(array.size for array in [*before, own])
    return pl.pallas_call(
        kernel,
        out_shape=jax.ShapeDtypeStruct((pairs, size // pairs) if before else own.shape, F32),
        in_specs=[pl.BlockSpec(memory_space=pltpu.VMEM)] * (1 + len(codes) + len(before)),
        out_specs=pl.BlockSpec(memory_space=pltpu.VMEM),
        compiler_params=pltpu.CompilerParams(vmem_limit_bytes=VMEM),
        cost_estimate=SMALL,
    )(own, *codes, *before)


def per_device(owners, cores, amplitudes, integral):
    pairs = amplitudes.shape[0]
    lines = owners // PLANE
    def swap(axis, size, array, by):
        return lax.ppermute(array, axis, [(i, i ^ by) for i in range(size)])

    plane = functools.partial(swap, "ab", owners)
    line = lambda array, by: swap("ab", owners, array, by * PLANE)
    core = functools.partial(swap, "cd", cores)

    unit = integral.shape[1] // UNITS
    early, late = (count * unit for count in AHEAD)

    halves = [amplitudes] + [core(amplitudes, j) for j in range(1, cores)]
    parts = split_by_plane(halves, lines)
    ready = [load(0, early, unit, integral, parts[0])]
    parts = [parts[0]] + [plane(parts[r], r) for r in range(1, PLANE)]
    parts = split_by_line(parts, cores, lines, pairs, ready[-1])
    ready.append(load(early, late, unit, integral, parts[0]))
    parts = [parts[0]] + [line(parts[s], s) for s in range(1, lines)]
    window = gather_window(parts, cores, pairs, ready[-1])

    start, more = early + late, MORE * unit
    own, *codes, chunk = product(window, integral, ready, start, STREAM * unit, more, unit, [])
    chunks = [[own] + [plane(code, r + 1) for r, code in enumerate(codes)]]
    start += STREAM * unit + more
    own, *codes = product(window, integral, [chunk], start, SECOND * unit - more, 0, unit, [own])
    chunks.append([own] + [plane(code, r + 1) for r, code in enumerate(codes)])
    sums = []
    for chunk in chunks:
        own, *codes = add_plane(chunk, lines, pairs)
        sums.append(add_line(own, [line(code, s + 1) for s, code in enumerate(codes)], sums, pairs))
    return sums[-1]


def solution(mesh):
    placed = (P("ab", None, "cd"), P("ab", "cd"))
    return jax.shard_map(
        functools.partial(per_device, mesh.shape["ab"], mesh.shape["cd"]),
        mesh=mesh,
        in_specs=placed,
        out_specs=P("ab", "cd"),
        check_vma=False,
    )
```

```python
import functools
import math

import jax
import jax.numpy as jnp
from jax import lax
from jax.experimental import pallas as pl
from jax.experimental.pallas import tpu as pltpu
from jax.sharding import PartitionSpec as P

F32, BF16 = jnp.float32, jnp.bfloat16
PLANE = 4
UNITS = 20
AHEAD = (2, 4, 1)
STREAM = 7
SECOND = 6
MORE = 3
SLOTS = 4
PIECES = 4
TILE = 512
MATRIX = 256
LANES = 128
TOP, TINY = 1440.0, 1e-30
SMALL = pl.CostEstimate(flops=1 << 20, bytes_accessed=1 << 20, transcendentals=0)
VMEM = 14 << 20


def select(rows, columns, source):
    row = lax.broadcasted_iota(jnp.int32, (rows, columns), 0)
    column = lax.broadcasted_iota(jnp.int32, (rows, columns), 1)
    return (column == source(row)).astype(BF16)


def copies(integral, start, unit, target, sems):
    step = target.shape[0] // PIECES
    return [
        pltpu.make_async_copy(
            integral.at[pl.ds(i * step, step), pl.ds(start, unit)],
            target.at[pl.ds(i * step, step), :],
            sems.at[i],
        )
        for i in range(PIECES)
    ]


def load(start, columns, unit, integral, after):
    depth = integral.shape[0]

    def kernel(integral_ref, after_ref, out_ref, sems):
        moves = []
        for k in range(columns // unit):
            target = out_ref.at[:, pl.ds(k * unit, unit)]
            moves += copies(integral_ref, start + k * unit, unit, target, sems.at[k])
        for move in moves:
            move.start()
        for move in moves:
            move.wait()

    return pl.pallas_call(
        kernel,
        out_shape=pltpu.VMEM((depth, columns), BF16),
        in_specs=[pl.BlockSpec(memory_space=pl.ANY)] * 2,
        out_specs=pl.BlockSpec(memory_space=pltpu.VMEM),
        scratch_shapes=[pltpu.SemaphoreType.DMA((columns // unit, PIECES))],
        compiler_params=pltpu.CompilerParams(vmem_limit_bytes=VMEM),
        cost_estimate=pl.CostEstimate(flops=0, bytes_accessed=depth * columns * 2, transcendentals=0),
    )(integral, after)


def encode(sums, largest):
    scale = (TOP / jnp.maximum(largest, TINY)).astype(BF16)
    scaled = sums * scale.astype(F32)
    square = scaled * scaled
    fourth = square * square
    return (fourth * fourth * square * (scaled * jnp.abs(scaled))).astype(BF16), scale


def decode(code, scale):
    code = code.astype(F32)
    size = jnp.exp2(jnp.log2(jnp.abs(code)) * (1.0 / 12.0)) * (1.0 / scale.astype(F32))
    return jnp.where(code < 0, -size, size)


def fold(group):
    return 8 // math.gcd(group, 8)


def window_row(row, group):
    whole = group // 8 * 8
    rest = group - whole
    if not rest:
        return row // group, row % group
    if not whole:
        return row // rest, row % rest
    behind = row - PLANE * whole
    tiled = behind < 0
    return jnp.where(tiled, row // whole, behind // rest), jnp.where(tiled, row % whole, whole + behind % rest)


def packed_rows(group, chip, part):
    whole = group // 8 * 8
    rest = group - whole
    rows = [(chip * whole, whole, part * whole)] if whole else []
    return rows + ([(PLANE * whole + chip * rest, rest, fold(group) * whole + part * rest)] if rest else [])


def unpacked(array, group, start, count):
    parts = fold(group)
    whole = group // 8 * 8
    rest = group - whole
    out = []
    for j in range(parts):
        pieces = []
        if start < whole:
            pieces.append(array[j * whole + start : j * whole + min(start + count, whole)])
        if start + count > whole:
            at = parts * whole + j * rest - whole
            pieces.append(array[at + max(start, whole) : at + start + count])
        out.append(pieces[0] if len(pieces) == 1 else jnp.concatenate(pieces, axis=0))
    return out


def split_by_plane(amplitudes, lines):
    pairs, blocks, offsets = amplitudes.shape
    group = lines * pairs

    def kernel(in_ref, *outs):
        me = lax.axis_index("ab")
        flat = in_ref[...].reshape(pairs * blocks, offsets)
        for r, out in enumerate(outs):

            def source(row):
                s, p = row // pairs, row % pairs
                return p * blocks + jnp.bitwise_xor(s * PLANE + r, me)

            taken = select(group, pairs * blocks, source)
            out[...] = jnp.dot(taken, flat, preferred_element_type=F32).astype(BF16)

    shape = jax.ShapeDtypeStruct((group, offsets), BF16)
    return pl.pallas_call(
        kernel,
        out_shape=[shape] * PLANE,
        in_specs=[pl.BlockSpec(memory_space=pltpu.VMEM)],
        out_specs=[pl.BlockSpec(memory_space=pltpu.VMEM)] * PLANE,
        compiler_params=pltpu.CompilerParams(vmem_limit_bytes=VMEM),
        cost_estimate=SMALL,
    )(amplitudes)


def split_by_line(parts, lines, pairs, after):
    group, offsets = parts[0].shape
    rows = PLANE * pairs

    def kernel(*refs):
        ins, outs = refs[:PLANE], refs[PLANE + 1 :]
        for s, out in enumerate(outs):
            total = 0.0
            for i, ref in enumerate(ins):
                r = (PLANE - i) % PLANE

                def source(row):
                    return jnp.where(row // pairs == r, s * pairs + row % pairs, -1)

                total += jnp.dot(select(rows, group, source), ref[...], preferred_element_type=F32)
            out[...] = total.astype(BF16)

    shape = jax.ShapeDtypeStruct((rows, offsets), BF16)
    return pl.pallas_call(
        kernel,
        out_shape=[shape] * lines,
        in_specs=[pl.BlockSpec(memory_space=pltpu.VMEM)] * PLANE + [pl.BlockSpec(memory_space=pl.ANY)],
        out_specs=[pl.BlockSpec(memory_space=pltpu.VMEM)] * lines,
        compiler_params=pltpu.CompilerParams(vmem_limit_bytes=VMEM),
        cost_estimate=SMALL,
    )(*parts, after)


def gather_half(parts, pairs, after):
    lines = len(parts)
    rows, offsets = parts[0].shape
    group = lines * pairs

    def kernel(*refs):
        total = 0.0
        for i in range(lines):
            s = (lines - i) % lines

            def source(row):
                r, at = window_row(row, group)
                return jnp.where(at // pairs == s, r * pairs + at % pairs, -1)

            total += jnp.dot(select(PLANE * group, rows, source), refs[i][...], preferred_element_type=F32)
        refs[-1][...] = total.astype(BF16)

    return pl.pallas_call(
        kernel,
        out_shape=jax.ShapeDtypeStruct((PLANE * group, offsets), BF16),
        in_specs=[pl.BlockSpec(memory_space=pltpu.VMEM)] * lines + [pl.BlockSpec(memory_space=pl.ANY)],
        out_specs=pl.BlockSpec(memory_space=pltpu.VMEM),
        compiler_params=pltpu.CompilerParams(vmem_limit_bytes=VMEM),
        cost_estimate=SMALL,
    )(*parts, after)


def join(halves, after):
    cores = len(halves)
    rows, offsets = halves[0].shape

    def kernel(*refs):
        core = lax.axis_index("cd")
        for c in range(cores):

            @pl.when(core == c)
            def _():
                for j in range(cores):
                    refs[-1][:, pl.ds((c ^ j) * offsets, offsets)] = refs[j][...]

    return pl.pallas_call(
        kernel,
        out_shape=jax.ShapeDtypeStruct((rows, cores * offsets), BF16),
        in_specs=[pl.BlockSpec(memory_space=pltpu.VMEM)] * cores + [pl.BlockSpec(memory_space=pl.ANY)],
        out_specs=pl.BlockSpec(memory_space=pltpu.VMEM),
        compiler_params=pltpu.CompilerParams(vmem_limit_bytes=VMEM),
        cost_estimate=SMALL,
    )(*halves, after)


def multiply(window_ref, chunk_ref, at, tile, sums):
    depth = window_ref.shape[1]
    if not sums:
        return [(0, jnp.dot(window_ref[...], chunk_ref[:, pl.ds(at, tile)], preferred_element_type=F32))]
    for k in range(depth // MATRIX):
        ks = pl.ds(k * MATRIX, MATRIX)
        for unit in range(2):
            pltpu.matmul_push_rhs(chunk_ref[ks, pl.ds(at + unit * MATRIX, MATRIX)], k % 2, unit)
        for unit in range(2):
            pltpu.matmul_acc_lhs(sums[unit], window_ref[:, ks], k % 2)
    return [(unit * MATRIX, pltpu.matmul_pop(sums[unit])) for unit in range(2)]


def product(window, integral, ready, start, stream, more, unit, after):
    group = window.shape[0] // PLANE
    depth = integral.shape[0]
    parts = fold(group)
    columns = sum(chunk.shape[1] for chunk in ready) + stream
    width = columns // parts
    tile = next(t for t in (TILE, 256, 128) if unit % t == 0)
    steps = stream // unit

    def kernel(window_ref, integral_ref, *refs):
        chunks, refs = refs[: len(ready)], refs[len(ready) + len(after) :]
        own, outs, refs = refs[0], refs[1:PLANE], refs[PLANE:]
        kept, ring, sems, more_sems = refs[-4:]
        incoming = [
            copies(integral_ref, start + k * unit, unit, ring.at[k % SLOTS], sems.at[k % SLOTS]) for k in range(steps)
        ]
        handed = [
            copies(integral_ref, start + stream + k * unit, unit, refs[0].at[:, pl.ds(k * unit, unit)], more_sems.at[k])
            for k in range(more // unit)
        ]
        for move in sum(incoming[: SLOTS - 1], []):
            move.start()

        def tiles(chunk_ref, column, sums):
            part, offset = divmod(column, width)
            for at in range(0, unit, tile):
                for place, values in multiply(window_ref, chunk_ref, at, tile, sums):
                    columns_at = pl.ds(offset + at + place, values.shape[1])
                    for r in range(PLANE):
                        target = own if r == 0 else kept.at[r - 1]
                        for begin, rows, where in packed_rows(group, r, part):
                            target[where : where + rows, columns_at] = values[begin : begin + rows]

        def work(*sums):
            sets = [sums[:2], sums[2:]]
            lead = len(held) if steps < SLOTS else 2
            for k in range(lead):
                tiles(held[k], k * unit, sets[k % 2])
            for k in range(max(len(held) - lead, steps)):
                if k < steps:
                    for move in incoming[k]:
                        move.wait()
                    for move in incoming[k + SLOTS - 1] if k + SLOTS - 1 < steps else []:
                        move.start()
                    tiles(ring.at[k % SLOTS], (len(held) + k) * unit, sets[0])
                if k + lead < len(held):
                    tiles(held[k + lead], (k + lead) * unit, sets[1])
                if k % 2 == 1 and k // 2 < len(handed):
                    for move in handed[k // 2]:
                        move.start()

        held = [
            chunk_ref.at[:, pl.ds(at, unit)] for chunk_ref in chunks for at in range(0, chunk_ref.shape[1], unit)
        ]
        rows = PLANE * group
        if tile == 2 * MATRIX and depth % MATRIX == 0 and rows % 16 == 0:
            pl.run_scoped(work, *[pltpu.ACC(i % 2)((rows, MATRIX), F32) for i in range(4)])
        else:
            work()

        largest = jnp.max(jnp.abs(kept[...]), axis=(0, 1, 2), keepdims=True)[0]
        for r, out in enumerate(outs):
            code, scale = encode(kept[r], largest)
            out[:, pl.ds(0, width)] = code
            out[:, pl.ds(width, LANES)] = jnp.broadcast_to(scale, (parts * group, LANES))
        for move in sum(handed, []):
            move.wait()

    shapes = [pltpu.VMEM((parts * group, width), F32)]
    shapes += [pltpu.VMEM((parts * group, width + LANES), BF16)] * (PLANE - 1)
    if more:
        shapes.append(pltpu.VMEM((depth, more), BF16))
    ready = [pltpu.with_memory_space_constraint(chunk, pltpu.VMEM) for chunk in ready]
    return pl.pallas_call(
        kernel,
        out_shape=shapes,
        in_specs=[pl.BlockSpec(memory_space=pltpu.VMEM), pl.BlockSpec(memory_space=pl.ANY)]
        + [pl.BlockSpec(memory_space=pltpu.VMEM)] * len(ready)
        + [pl.BlockSpec(memory_space=pl.ANY)] * len(after),
        out_specs=[pl.BlockSpec(memory_space=pltpu.VMEM)] * len(shapes),
        scratch_shapes=[
            pltpu.VMEM((PLANE - 1, parts * group, width), F32),
            pltpu.VMEM((min(SLOTS, steps), depth, unit), BF16),
            pltpu.SemaphoreType.DMA((min(SLOTS, steps), PIECES)),
            pltpu.SemaphoreType.DMA((max(more // unit, 1), PIECES)),
        ],
        compiler_params=pltpu.CompilerParams(vmem_limit_bytes=VMEM),
        cost_estimate=pl.CostEstimate(
            flops=2 * window.shape[0] * depth * columns, bytes_accessed=depth * columns * 2, transcendentals=0
        ),
    )(window, integral, *ready, *after)


def add_codes(chunk):
    rows, width = chunk[0].shape

    def kernel(own_ref, *refs):
        total = own_ref[...]
        for ref in refs[:-1]:
            total += decode(ref[:, pl.ds(0, width)], ref[:, pl.ds(width, 1)])
        refs[-1][...] = total

    return pl.pallas_call(
        kernel,
        out_shape=jax.ShapeDtypeStruct((rows, width), F32),
        in_specs=[pl.BlockSpec(memory_space=pltpu.VMEM)] * len(chunk),
        out_specs=pl.BlockSpec(memory_space=pltpu.VMEM),
        compiler_params=pltpu.CompilerParams(vmem_limit_bytes=VMEM),
        cost_estimate=SMALL,
    )(*chunk)


def line_fold(widths, parts):
    return next(n for n in (8, 4, 2, 1) if n * parts <= 8 and all(width % (n * LANES) == 0 for width in widths))


def add_plane(chunks, lines, pairs):
    group = lines * pairs
    parts = fold(group)
    widths = [own.shape[1] for own, *_ in chunks]
    pieces = line_fold(widths, parts)
    rows, columns = parts * pieces * pairs, sum(widths) // pieces

    def kernel(*refs):
        ins, own, outs, kept = list(refs[: -lines - 1]), refs[-lines - 1], refs[-lines:-1], refs[-1]
        start, largest = 0, jnp.zeros((1, 1), F32)
        for i, width in enumerate(widths):
            total = ins.pop(0)[...]
            for _ in chunks[i][1:]:
                ref = ins.pop(0)
                total += decode(ref[:, pl.ds(0, width)], ref[:, pl.ds(width, 1)])
            largest = jnp.maximum(largest, jnp.max(jnp.abs(total), keepdims=True))
            piece = width // pieces
            for s in range(lines):
                for j, part in enumerate(unpacked(total, group, s * pairs, pairs)):
                    for k in range(pieces):
                        row = pl.ds((j * pieces + k) * pairs, pairs)
                        value = part[:, k * piece : (k + 1) * piece]
                        if s == 0:
                            own[row, pl.ds(start, piece)] = value
                        else:
                            kept[s - 1, row, pl.ds(start, piece)] = value
            start += piece
        for s, out in enumerate(outs):
            code, scale = encode(kept[s], largest)
            out[:, pl.ds(0, columns)] = code
            out[:, pl.ds(columns, LANES)] = jnp.broadcast_to(scale, (rows, LANES))

    code = jax.ShapeDtypeStruct((rows, columns + LANES), BF16)
    return pl.pallas_call(
        kernel,
        out_shape=[jax.ShapeDtypeStruct((rows, columns), F32)] + [code] * (lines - 1),
        in_specs=[pl.BlockSpec(memory_space=pltpu.VMEM)] * sum(map(len, chunks)),
        out_specs=[pl.BlockSpec(memory_space=pltpu.VMEM)] * lines,
        scratch_shapes=[pltpu.VMEM((lines - 1, rows, columns), F32)],
        compiler_params=pltpu.CompilerParams(vmem_limit_bytes=VMEM),
        cost_estimate=SMALL,
    )(*[ref for chunk in chunks for ref in chunk])


def add_line(own, codes, widths, parts, pairs):
    rows, columns = own.shape
    pieces = line_fold(widths, parts)

    def kernel(own_ref, *refs):
        total = own_ref[...]
        for ref in refs[:-1]:
            total += decode(ref[:, pl.ds(0, columns)], ref[:, pl.ds(columns, 1)])
        at, start = 0, 0
        for width in widths:
            piece = width // pieces
            for j in range(parts * pieces):
                refs[-1][:, pl.ds(start, piece)] = total[j * pairs : (j + 1) * pairs, at : at + piece]
                start += piece
            at += piece

    return pl.pallas_call(
        kernel,
        out_shape=jax.ShapeDtypeStruct((pairs, sum(widths) * parts), F32),
        in_specs=[pl.BlockSpec(memory_space=pltpu.VMEM)] * (1 + len(codes)),
        out_specs=pl.BlockSpec(memory_space=pltpu.VMEM),
        compiler_params=pltpu.CompilerParams(vmem_limit_bytes=VMEM),
        cost_estimate=SMALL,
    )(own, *codes)


def per_device(owners, cores, amplitudes, integral):
    pairs = amplitudes.shape[0]
    lines = owners // PLANE
    def swap(axis, size, array, by):
        return lax.ppermute(array, axis, [(i, i ^ by) for i in range(size)])

    def farthest_first(exchange, arrays):
        return [exchange(array, i + 1) for i, array in enumerate(arrays)][::-1]

    plane = functools.partial(swap, "ab", owners)
    line = lambda array, by: swap("ab", owners, array, by * PLANE)
    core = functools.partial(swap, "cd", cores)

    unit = integral.shape[1] // UNITS
    early, middle, late = (count * unit for count in AHEAD)

    parts = split_by_plane(amplitudes, lines)
    ready = [load(0, early, unit, integral, parts[0])]
    parts = [parts[0]] + farthest_first(plane, parts[1:])
    parts = split_by_line(parts, lines, pairs, ready[-1])
    ready.append(load(early, middle, unit, integral, parts[0]))
    parts = [parts[0]] + farthest_first(line, parts[1:])
    half = gather_half(parts, pairs, ready[-1])
    ready.append(load(early + middle, late, unit, integral, half))
    window = join([half] + [core(half, j) for j in range(1, cores)], ready[-1])

    start, more = early + middle + late, MORE * unit
    own, *codes, chunk = product(window, integral, ready, start, STREAM * unit, more, unit, [])
    chunks = [[own] + farthest_first(plane, codes)]
    start += STREAM * unit + more
    own, *codes = product(window, integral, [chunk], start, SECOND * unit - more, 0, unit, [own])
    chunks.append([own] + farthest_first(plane, codes))
    chunks[0] = [add_codes(chunks[0])]
    own, *codes = add_plane(chunks, lines, pairs)
    codes = farthest_first(line, codes)
    return add_line(own, codes, [chunk[0].shape[1] for chunk in chunks], fold(lines * pairs), pairs)


def solution(mesh):
    placed = (P("ab", None, "cd"), P("ab", "cd"))
    return jax.shard_map(
        functools.partial(per_device, mesh.shape["ab"], mesh.shape["cd"]),
        mesh=mesh,
        in_specs=placed,
        out_specs=P("ab", "cd"),
        check_vma=False,
    )
```

```python
import functools
import math

import jax
import jax.numpy as jnp
from jax import lax
from jax.experimental import pallas as pl
from jax.experimental.pallas import tpu as pltpu
from jax.sharding import PartitionSpec as P

F32, BF16 = jnp.float32, jnp.bfloat16
PLANE = 4
UNITS = 20
AHEAD = (2, 4, 1)
STREAM = 7
SECOND = 6
MORE = 3
SLOTS = 4
PIECES = 4
TILE = 512
MATRIX = 256
LANES = 128
TOP, TINY = 1440.0, 1e-30
SMALL = pl.CostEstimate(flops=1 << 20, bytes_accessed=1 << 20, transcendentals=0)
VMEM = 14 << 20


def select(rows, columns, source):
    row = lax.broadcasted_iota(jnp.int32, (rows, columns), 0)
    column = lax.broadcasted_iota(jnp.int32, (rows, columns), 1)
    return (column == source(row)).astype(BF16)


def copies(integral, start, unit, target, sems):
    step = target.shape[0] // PIECES
    return [
        pltpu.make_async_copy(
            integral.at[pl.ds(i * step, step), pl.ds(start, unit)],
            target.at[pl.ds(i * step, step), :],
            sems.at[i],
        )
        for i in range(PIECES)
    ]


def load(start, columns, unit, integral, after):
    depth = integral.shape[0]

    def kernel(integral_ref, after_ref, out_ref, sems):
        moves = []
        for k in range(columns // unit):
            target = out_ref.at[:, pl.ds(k * unit, unit)]
            moves += copies(integral_ref, start + k * unit, unit, target, sems.at[k])
        for move in moves:
            move.start()
        for move in moves:
            move.wait()

    return pl.pallas_call(
        kernel,
        out_shape=pltpu.VMEM((depth, columns), BF16),
        in_specs=[pl.BlockSpec(memory_space=pl.ANY)] * 2,
        out_specs=pl.BlockSpec(memory_space=pltpu.VMEM),
        scratch_shapes=[pltpu.SemaphoreType.DMA((columns // unit, PIECES))],
        compiler_params=pltpu.CompilerParams(vmem_limit_bytes=VMEM),
        cost_estimate=pl.CostEstimate(flops=0, bytes_accessed=depth * columns * 2, transcendentals=0),
    )(integral, after)


def encode(sums, largest):
    scale = (TOP / jnp.maximum(largest, TINY)).astype(BF16)
    scaled = sums * scale.astype(F32)
    square = scaled * scaled
    fourth = square * square
    return (fourth * fourth * square * (scaled * jnp.abs(scaled))).astype(BF16), scale


def decode(code, scale):
    code = code.astype(F32)
    size = jnp.exp2(jnp.log2(jnp.abs(code)) * (1.0 / 12.0)) * (1.0 / scale.astype(F32))
    return jnp.where(code < 0, -size, size)


def fold(group):
    return 8 // math.gcd(group, 8)


def window_row(row, group):
    whole = group // 8 * 8
    rest = group - whole
    if not rest:
        return row // group, row % group
    if not whole:
        return row // rest, row % rest
    behind = row - PLANE * whole
    tiled = behind < 0
    return jnp.where(tiled, row // whole, behind // rest), jnp.where(tiled, row % whole, whole + behind % rest)


def packed_rows(group, chip, part):
    whole = group // 8 * 8
    rest = group - whole
    rows = [(chip * whole, whole, part * whole)] if whole else []
    return rows + ([(PLANE * whole + chip * rest, rest, fold(group) * whole + part * rest)] if rest else [])


def unpacked(array, group, start, count):
    parts = fold(group)
    whole = group // 8 * 8
    rest = group - whole
    out = []
    for j in range(parts):
        pieces = []
        if start < whole:
            pieces.append(array[j * whole + start : j * whole + min(start + count, whole)])
        if start + count > whole:
            at = parts * whole + j * rest - whole
            pieces.append(array[at + max(start, whole) : at + start + count])
        out.append(pieces[0] if len(pieces) == 1 else jnp.concatenate(pieces, axis=0))
    return out


def split_by_plane(amplitudes, lines):
    pairs, blocks, offsets = amplitudes.shape
    group = lines * pairs

    def kernel(in_ref, *outs):
        me = lax.axis_index("ab")
        flat = in_ref[...].reshape(pairs * blocks, offsets)
        for r, out in enumerate(outs):

            def source(row):
                s, p = row // pairs, row % pairs
                return p * blocks + jnp.bitwise_xor(s * PLANE + r, me)

            taken = select(group, pairs * blocks, source)
            out[...] = jnp.dot(taken, flat, preferred_element_type=F32).astype(BF16)

    shape = jax.ShapeDtypeStruct((group, offsets), BF16)
    return pl.pallas_call(
        kernel,
        out_shape=[shape] * PLANE,
        in_specs=[pl.BlockSpec(memory_space=pltpu.VMEM)],
        out_specs=[pl.BlockSpec(memory_space=pltpu.VMEM)] * PLANE,
        compiler_params=pltpu.CompilerParams(vmem_limit_bytes=VMEM),
        cost_estimate=SMALL,
    )(amplitudes)


def split_by_line(parts, lines, pairs, after):
    group, offsets = parts[0].shape
    rows = PLANE * pairs

    def kernel(*refs):
        ins, outs = refs[:PLANE], refs[PLANE + 1 :]
        for s, out in enumerate(outs):
            total = 0.0
            for i, ref in enumerate(ins):
                r = (PLANE - i) % PLANE

                def source(row):
                    return jnp.where(row // pairs == r, s * pairs + row % pairs, -1)

                total += jnp.dot(select(rows, group, source), ref[...], preferred_element_type=F32)
            out[...] = total.astype(BF16)

    shape = jax.ShapeDtypeStruct((rows, offsets), BF16)
    return pl.pallas_call(
        kernel,
        out_shape=[shape] * lines,
        in_specs=[pl.BlockSpec(memory_space=pltpu.VMEM)] * PLANE + [pl.BlockSpec(memory_space=pl.ANY)],
        out_specs=[pl.BlockSpec(memory_space=pltpu.VMEM)] * lines,
        compiler_params=pltpu.CompilerParams(vmem_limit_bytes=VMEM),
        cost_estimate=SMALL,
    )(*parts, after)


def gather_half(parts, pairs, after):
    lines = len(parts)
    rows, offsets = parts[0].shape
    group = lines * pairs

    def kernel(*refs):
        total = 0.0
        for i in range(lines):
            s = (lines - i) % lines

            def source(row):
                r, at = window_row(row, group)
                return jnp.where(at // pairs == s, r * pairs + at % pairs, -1)

            total += jnp.dot(select(PLANE * group, rows, source), refs[i][...], preferred_element_type=F32)
        refs[-1][...] = total.astype(BF16)

    return pl.pallas_call(
        kernel,
        out_shape=jax.ShapeDtypeStruct((PLANE * group, offsets), BF16),
        in_specs=[pl.BlockSpec(memory_space=pltpu.VMEM)] * lines + [pl.BlockSpec(memory_space=pl.ANY)],
        out_specs=pl.BlockSpec(memory_space=pltpu.VMEM),
        compiler_params=pltpu.CompilerParams(vmem_limit_bytes=VMEM),
        cost_estimate=SMALL,
    )(*parts, after)


def join(halves, after):
    cores = len(halves)
    rows, offsets = halves[0].shape

    def kernel(*refs):
        core = lax.axis_index("cd")
        for c in range(cores):

            @pl.when(core == c)
            def _():
                for j in range(cores):
                    refs[-1][:, pl.ds((c ^ j) * offsets, offsets)] = refs[j][...]

    return pl.pallas_call(
        kernel,
        out_shape=jax.ShapeDtypeStruct((rows, cores * offsets), BF16),
        in_specs=[pl.BlockSpec(memory_space=pltpu.VMEM)] * cores + [pl.BlockSpec(memory_space=pl.ANY)],
        out_specs=pl.BlockSpec(memory_space=pltpu.VMEM),
        compiler_params=pltpu.CompilerParams(vmem_limit_bytes=VMEM),
        cost_estimate=SMALL,
    )(*halves, after)


def multiply(window_ref, chunk_ref, at, tile, sums):
    depth = window_ref.shape[1]
    if not sums:
        return [(0, jnp.dot(window_ref[...], chunk_ref[:, pl.ds(at, tile)], preferred_element_type=F32))]
    for k in range(depth // MATRIX):
        ks = pl.ds(k * MATRIX, MATRIX)
        for unit in range(2):
            pltpu.matmul_push_rhs(chunk_ref[ks, pl.ds(at + unit * MATRIX, MATRIX)], k % 2, unit)
        for unit in range(2):
            pltpu.matmul_acc_lhs(sums[unit], window_ref[:, ks], k % 2)
    return [(unit * MATRIX, pltpu.matmul_pop(sums[unit])) for unit in range(2)]


def product(window, integral, ready, start, stream, more, unit, after):
    group = window.shape[0] // PLANE
    depth = integral.shape[0]
    parts = fold(group)
    columns = sum(chunk.shape[1] for chunk in ready) + stream
    width = columns // parts
    tile = next(t for t in (TILE, 256, 128) if unit % t == 0)
    steps = stream // unit

    def kernel(window_ref, integral_ref, *refs):
        chunks, refs = refs[: len(ready)], refs[len(ready) + len(after) :]
        own, outs, refs = refs[0], refs[1:PLANE], refs[PLANE:]
        kept, ring, sems, more_sems = refs[-4:]
        incoming = [
            copies(integral_ref, start + k * unit, unit, ring.at[k % SLOTS], sems.at[k % SLOTS]) for k in range(steps)
        ]
        handed = [
            copies(integral_ref, start + stream + k * unit, unit, refs[0].at[:, pl.ds(k * unit, unit)], more_sems.at[k])
            for k in range(more // unit)
        ]
        ahead = min(SLOTS - 1, steps)
        for move in incoming[0]:
            move.start()

        def tiles(chunk_ref, column, sums):
            part, offset = divmod(column, width)
            for at in range(0, unit, tile):
                for place, values in multiply(window_ref, chunk_ref, at, tile, sums):
                    columns_at = pl.ds(offset + at + place, values.shape[1])
                    for r in range(PLANE):
                        target = own if r == 0 else kept.at[r - 1]
                        for begin, rows, where in packed_rows(group, r, part):
                            target[where : where + rows, columns_at] = values[begin : begin + rows]

        def work(*sums):
            sets = [sums[:2], sums[2:]]
            lead = len(held) if steps < SLOTS else 2
            for k in range(lead):
                tiles(held[k], k * unit, sets[k % 2])
                for move in incoming[k + 1] if k + 1 < ahead else []:
                    move.start()
            for k in range(max(len(held) - lead, steps)):
                if k < steps:
                    for move in incoming[k]:
                        move.wait()
                    for move in incoming[k + SLOTS - 1] if k + SLOTS - 1 < steps else []:
                        move.start()
                    tiles(ring.at[k % SLOTS], (len(held) + k) * unit, sets[0])
                if k + lead < len(held):
                    tiles(held[k + lead], (k + lead) * unit, sets[1])
                if k % 2 == 1 and k // 2 < len(handed):
                    for move in handed[k // 2]:
                        move.start()

        held = [
            chunk_ref.at[:, pl.ds(at, unit)] for chunk_ref in chunks for at in range(0, chunk_ref.shape[1], unit)
        ]
        rows = PLANE * group
        if tile == 2 * MATRIX and depth % MATRIX == 0 and rows % 16 == 0:
            pl.run_scoped(work, *[pltpu.ACC(i % 2)((rows, MATRIX), F32) for i in range(4)])
        else:
            work()

        largest = jnp.max(jnp.abs(kept[...]), axis=(0, 1, 2), keepdims=True)[0]
        for r, out in enumerate(outs):
            code, scale = encode(kept[r], largest)
            out[:, pl.ds(0, width)] = code
            out[:, pl.ds(width, LANES)] = jnp.broadcast_to(scale, (parts * group, LANES))
        for move in sum(handed, []):
            move.wait()

    shapes = [pltpu.VMEM((parts * group, width), F32)]
    shapes += [pltpu.VMEM((parts * group, width + LANES), BF16)] * (PLANE - 1)
    if more:
        shapes.append(pltpu.VMEM((depth, more), BF16))
    ready = [pltpu.with_memory_space_constraint(chunk, pltpu.VMEM) for chunk in ready]
    return pl.pallas_call(
        kernel,
        out_shape=shapes,
        in_specs=[pl.BlockSpec(memory_space=pltpu.VMEM), pl.BlockSpec(memory_space=pl.ANY)]
        + [pl.BlockSpec(memory_space=pltpu.VMEM)] * len(ready)
        + [pl.BlockSpec(memory_space=pl.ANY)] * len(after),
        out_specs=[pl.BlockSpec(memory_space=pltpu.VMEM)] * len(shapes),
        scratch_shapes=[
            pltpu.VMEM((PLANE - 1, parts * group, width), F32),
            pltpu.VMEM((min(SLOTS, steps), depth, unit), BF16),
            pltpu.SemaphoreType.DMA((min(SLOTS, steps), PIECES)),
            pltpu.SemaphoreType.DMA((max(more // unit, 1), PIECES)),
        ],
        compiler_params=pltpu.CompilerParams(vmem_limit_bytes=VMEM),
        cost_estimate=pl.CostEstimate(
            flops=2 * window.shape[0] * depth * columns, bytes_accessed=depth * columns * 2, transcendentals=0
        ),
    )(window, integral, *ready, *after)


def add_codes(chunk):
    rows, width = chunk[0].shape

    def kernel(own_ref, *refs):
        total = own_ref[...]
        for ref in refs[:-1]:
            total += decode(ref[:, pl.ds(0, width)], ref[:, pl.ds(width, 1)])
        refs[-1][...] = total

    return pl.pallas_call(
        kernel,
        out_shape=jax.ShapeDtypeStruct((rows, width), F32),
        in_specs=[pl.BlockSpec(memory_space=pltpu.VMEM)] * len(chunk),
        out_specs=pl.BlockSpec(memory_space=pltpu.VMEM),
        compiler_params=pltpu.CompilerParams(vmem_limit_bytes=VMEM),
        cost_estimate=SMALL,
    )(*chunk)


def line_fold(widths, parts):
    return next(n for n in (8, 4, 2, 1) if n * parts <= 8 and all(width % (n * LANES) == 0 for width in widths))


def add_plane(chunks, lines, pairs):
    group = lines * pairs
    parts = fold(group)
    widths = [own.shape[1] for own, *_ in chunks]
    pieces = line_fold(widths, parts)
    rows, columns = parts * pieces * pairs, sum(widths) // pieces

    def kernel(*refs):
        ins, own, outs, kept = list(refs[: -lines - 1]), refs[-lines - 1], refs[-lines:-1], refs[-1]
        start, largest = 0, jnp.zeros((1, 1), F32)
        for i, width in enumerate(widths):
            total = ins.pop(0)[...]
            for _ in chunks[i][1:]:
                ref = ins.pop(0)
                total += decode(ref[:, pl.ds(0, width)], ref[:, pl.ds(width, 1)])
            largest = jnp.maximum(largest, jnp.max(jnp.abs(total), keepdims=True))
            piece = width // pieces
            for s in range(lines):
                for j, part in enumerate(unpacked(total, group, s * pairs, pairs)):
                    for k in range(pieces):
                        row = pl.ds((j * pieces + k) * pairs, pairs)
                        value = part[:, k * piece : (k + 1) * piece]
                        if s == 0:
                            own[row, pl.ds(start, piece)] = value
                        else:
                            kept[s - 1, row, pl.ds(start, piece)] = value
            start += piece
        for s, out in enumerate(outs):
            code, scale = encode(kept[s], largest)
            out[:, pl.ds(0, columns)] = code
            out[:, pl.ds(columns, LANES)] = jnp.broadcast_to(scale, (rows, LANES))

    code = jax.ShapeDtypeStruct((rows, columns + LANES), BF16)
    return pl.pallas_call(
        kernel,
        out_shape=[jax.ShapeDtypeStruct((rows, columns), F32)] + [code] * (lines - 1),
        in_specs=[pl.BlockSpec(memory_space=pltpu.VMEM)] * sum(map(len, chunks)),
        out_specs=[pl.BlockSpec(memory_space=pltpu.VMEM)] * lines,
        scratch_shapes=[pltpu.VMEM((lines - 1, rows, columns), F32)],
        compiler_params=pltpu.CompilerParams(vmem_limit_bytes=VMEM),
        cost_estimate=SMALL,
    )(*[ref for chunk in chunks for ref in chunk])


def add_line(own, codes, widths, parts, pairs):
    rows, columns = own.shape
    pieces = line_fold(widths, parts)

    def kernel(own_ref, *refs):
        total = own_ref[...]
        for ref in refs[:-1]:
            total += decode(ref[:, pl.ds(0, columns)], ref[:, pl.ds(columns, 1)])
        at, start = 0, 0
        for width in widths:
            piece = width // pieces
            for j in range(parts * pieces):
                refs[-1][:, pl.ds(start, piece)] = total[j * pairs : (j + 1) * pairs, at : at + piece]
                start += piece
            at += piece

    return pl.pallas_call(
        kernel,
        out_shape=jax.ShapeDtypeStruct((pairs, sum(widths) * parts), F32),
        in_specs=[pl.BlockSpec(memory_space=pltpu.VMEM)] * (1 + len(codes)),
        out_specs=pl.BlockSpec(memory_space=pltpu.VMEM),
        compiler_params=pltpu.CompilerParams(vmem_limit_bytes=VMEM),
        cost_estimate=SMALL,
    )(own, *codes)


def per_device(owners, cores, amplitudes, integral):
    pairs = amplitudes.shape[0]
    lines = owners // PLANE
    def swap(axis, size, array, by):
        return lax.ppermute(array, axis, [(i, i ^ by) for i in range(size)])

    def farthest_first(exchange, arrays):
        return [exchange(array, i + 1) for i, array in enumerate(arrays)][::-1]

    plane = functools.partial(swap, "ab", owners)
    line = lambda array, by: swap("ab", owners, array, by * PLANE)
    core = functools.partial(swap, "cd", cores)

    unit = integral.shape[1] // UNITS
    early, middle, late = (count * unit for count in AHEAD)

    parts = split_by_plane(amplitudes, lines)
    ready = [load(0, early, unit, integral, parts[0])]
    parts = [parts[0]] + farthest_first(plane, parts[1:])
    parts = split_by_line(parts, lines, pairs, ready[-1])
    ready.append(load(early, middle, unit, integral, parts[0]))
    parts = [parts[0]] + farthest_first(line, parts[1:])
    half = gather_half(parts, pairs, ready[-1])
    ready.append(load(early + middle, late, unit, integral, half))
    window = join([half] + [core(half, j) for j in range(1, cores)], ready[-1])

    start, more = early + middle + late, MORE * unit
    own, *codes, chunk = product(window, integral, ready, start, STREAM * unit, more, unit, [])
    chunks = [[own] + farthest_first(plane, codes)]
    start += STREAM * unit + more
    own, *codes = product(window, integral, [chunk], start, SECOND * unit - more, 0, unit, [own])
    chunks.append([own] + farthest_first(plane, codes))
    chunks[0] = [add_codes(chunks[0])]
    own, *codes = add_plane(chunks, lines, pairs)
    codes = farthest_first(line, codes)
    return add_line(own, codes, [chunk[0].shape[1] for chunk in chunks], fold(lines * pairs), pairs)


def solution(mesh):
    placed = (P("ab", None, "cd"), P("ab", "cd"))
    return jax.shard_map(
        functools.partial(per_device, mesh.shape["ab"], mesh.shape["cd"]),
        mesh=mesh,
        in_specs=placed,
        out_specs=P("ab", "cd"),
        check_vma=False,
    )
```

```python
import functools
import math

import jax
import jax.numpy as jnp
from jax import lax
from jax.experimental import pallas as pl
from jax.experimental.pallas import tpu as pltpu
from jax.sharding import PartitionSpec as P

F32, BF16 = jnp.float32, jnp.bfloat16
PLANE = 4
UNITS = 20
AHEAD = (2, 4, 1)
STREAM = 7
SECOND = 6
MORE = 3
SLOTS = 4
PIECES = 4
TILE = 512
MATRIX = 256
LANES = 128
TOP, TINY = 1440.0, 1e-30
SMALL = pl.CostEstimate(flops=1 << 20, bytes_accessed=1 << 20, transcendentals=0)
VMEM = 14 << 20


def select(rows, columns, source):
    row = lax.broadcasted_iota(jnp.int32, (rows, columns), 0)
    column = lax.broadcasted_iota(jnp.int32, (rows, columns), 1)
    return (column == source(row)).astype(BF16)


def copies(integral, start, unit, target, sems):
    step = target.shape[0] // PIECES
    return [
        pltpu.make_async_copy(
            integral.at[pl.ds(i * step, step), pl.ds(start, unit)],
            target.at[pl.ds(i * step, step), :],
            sems.at[i],
        )
        for i in range(PIECES)
    ]


def load(start, columns, unit, integral, after):
    depth = integral.shape[0]

    def kernel(integral_ref, after_ref, out_ref, sems):
        moves = []
        for k in range(columns // unit):
            target = out_ref.at[:, pl.ds(k * unit, unit)]
            moves += copies(integral_ref, start + k * unit, unit, target, sems.at[k])
        for move in moves:
            move.start()
        for move in moves:
            move.wait()

    return pl.pallas_call(
        kernel,
        out_shape=pltpu.VMEM((depth, columns), BF16),
        in_specs=[pl.BlockSpec(memory_space=pl.ANY)] * 2,
        out_specs=pl.BlockSpec(memory_space=pltpu.VMEM),
        scratch_shapes=[pltpu.SemaphoreType.DMA((columns // unit, PIECES))],
        compiler_params=pltpu.CompilerParams(vmem_limit_bytes=VMEM),
        cost_estimate=pl.CostEstimate(flops=0, bytes_accessed=depth * columns * 2, transcendentals=0),
    )(integral, after)


def encode(sums, largest):
    scale = (TOP / jnp.maximum(largest, TINY)).astype(BF16)
    scaled = sums * scale.astype(F32)
    square = scaled * scaled
    fourth = square * square
    return (fourth * fourth * square * (scaled * jnp.abs(scaled))).astype(BF16), scale


def decode(code, scale):
    code = code.astype(F32)
    size = jnp.exp2(jnp.log2(jnp.abs(code)) * (1.0 / 12.0)) * (1.0 / scale.astype(F32))
    return jnp.where(code < 0, -size, size)


def fold(group):
    return 8 // math.gcd(group, 8)


def window_row(row, group):
    whole = group // 8 * 8
    rest = group - whole
    if not rest:
        return row // group, row % group
    if not whole:
        return row // rest, row % rest
    behind = row - PLANE * whole
    tiled = behind < 0
    return jnp.where(tiled, row // whole, behind // rest), jnp.where(tiled, row % whole, whole + behind % rest)


def packed_rows(group, chip, part):
    whole = group // 8 * 8
    rest = group - whole
    rows = [(chip * whole, whole, part * whole)] if whole else []
    return rows + ([(PLANE * whole + chip * rest, rest, fold(group) * whole + part * rest)] if rest else [])


def unpacked(array, group, start, count):
    parts = fold(group)
    whole = group // 8 * 8
    rest = group - whole
    out = []
    for j in range(parts):
        pieces = []
        if start < whole:
            pieces.append(array[j * whole + start : j * whole + min(start + count, whole)])
        if start + count > whole:
            at = parts * whole + j * rest - whole
            pieces.append(array[at + max(start, whole) : at + start + count])
        out.append(pieces[0] if len(pieces) == 1 else jnp.concatenate(pieces, axis=0))
    return out


def split_by_plane(amplitudes, lines):
    pairs, blocks, offsets = amplitudes.shape
    group = lines * pairs

    def kernel(in_ref, *outs):
        me = lax.axis_index("ab")
        flat = in_ref[...].reshape(pairs * blocks, offsets)
        for r, out in enumerate(outs):

            def source(row):
                s, p = row // pairs, row % pairs
                return p * blocks + jnp.bitwise_xor(s * PLANE + r, me)

            taken = select(group, pairs * blocks, source)
            out[...] = jnp.dot(taken, flat, preferred_element_type=F32).astype(BF16)

    shape = jax.ShapeDtypeStruct((group, offsets), BF16)
    return pl.pallas_call(
        kernel,
        out_shape=[shape] * PLANE,
        in_specs=[pl.BlockSpec(memory_space=pltpu.VMEM)],
        out_specs=[pl.BlockSpec(memory_space=pltpu.VMEM)] * PLANE,
        compiler_params=pltpu.CompilerParams(vmem_limit_bytes=VMEM),
        cost_estimate=SMALL,
    )(amplitudes)


def split_by_line(parts, lines, pairs, after):
    group, offsets = parts[0].shape
    rows = PLANE * pairs

    def kernel(*refs):
        ins, outs = refs[:PLANE], refs[PLANE + 1 :]
        for s, out in enumerate(outs):
            total = 0.0
            for i, ref in enumerate(ins):
                r = (PLANE - i) % PLANE

                def source(row):
                    return jnp.where(row // pairs == r, s * pairs + row % pairs, -1)

                total += jnp.dot(select(rows, group, source), ref[...], preferred_element_type=F32)
            out[...] = total.astype(BF16)

    shape = jax.ShapeDtypeStruct((rows, offsets), BF16)
    return pl.pallas_call(
        kernel,
        out_shape=[shape] * lines,
        in_specs=[pl.BlockSpec(memory_space=pltpu.VMEM)] * PLANE + [pl.BlockSpec(memory_space=pl.ANY)],
        out_specs=[pl.BlockSpec(memory_space=pltpu.VMEM)] * lines,
        compiler_params=pltpu.CompilerParams(vmem_limit_bytes=VMEM),
        cost_estimate=SMALL,
    )(*parts, after)


def gather_half(parts, pairs, after):
    lines = len(parts)
    rows, offsets = parts[0].shape
    group = lines * pairs

    def kernel(*refs):
        total = 0.0
        for i in range(lines):
            s = (lines - i) % lines

            def source(row):
                r, at = window_row(row, group)
                return jnp.where(at // pairs == s, r * pairs + at % pairs, -1)

            total += jnp.dot(select(PLANE * group, rows, source), refs[i][...], preferred_element_type=F32)
        refs[-1][...] = total.astype(BF16)

    return pl.pallas_call(
        kernel,
        out_shape=jax.ShapeDtypeStruct((PLANE * group, offsets), BF16),
        in_specs=[pl.BlockSpec(memory_space=pltpu.VMEM)] * lines + [pl.BlockSpec(memory_space=pl.ANY)],
        out_specs=pl.BlockSpec(memory_space=pltpu.VMEM),
        compiler_params=pltpu.CompilerParams(vmem_limit_bytes=VMEM),
        cost_estimate=SMALL,
    )(*parts, after)


def join(halves, after):
    cores = len(halves)
    rows, offsets = halves[0].shape

    def kernel(*refs):
        core = lax.axis_index("cd")
        for c in range(cores):

            @pl.when(core == c)
            def _():
                for j in range(cores):
                    refs[-1][:, pl.ds((c ^ j) * offsets, offsets)] = refs[j][...]

    return pl.pallas_call(
        kernel,
        out_shape=jax.ShapeDtypeStruct((rows, cores * offsets), BF16),
        in_specs=[pl.BlockSpec(memory_space=pltpu.VMEM)] * cores + [pl.BlockSpec(memory_space=pl.ANY)],
        out_specs=pl.BlockSpec(memory_space=pltpu.VMEM),
        compiler_params=pltpu.CompilerParams(vmem_limit_bytes=VMEM),
        cost_estimate=SMALL,
    )(*halves, after)


def multiply(window_ref, chunk_ref, at, tile, sums):
    depth = window_ref.shape[1]
    if not sums:
        return [(0, jnp.dot(window_ref[...], chunk_ref[:, pl.ds(at, tile)], preferred_element_type=F32))]
    for k in range(depth // MATRIX):
        ks = pl.ds(k * MATRIX, MATRIX)
        for unit in range(2):
            pltpu.matmul_push_rhs(chunk_ref[ks, pl.ds(at + unit * MATRIX, MATRIX)], k % 2, unit)
        for unit in range(2):
            pltpu.matmul_acc_lhs(sums[unit], window_ref[:, ks], k % 2)
    return [(unit * MATRIX, pltpu.matmul_pop(sums[unit])) for unit in range(2)]


def product(window, integral, ready, start, stream, more, unit, after):
    group = window.shape[0] // PLANE
    depth = integral.shape[0]
    parts = fold(group)
    columns = sum(chunk.shape[1] for chunk in ready) + stream
    width = columns // parts
    tile = next(t for t in (TILE, 256, 128) if unit % t == 0)
    steps = stream // unit

    def kernel(window_ref, integral_ref, *refs):
        chunks, refs = refs[: len(ready)], refs[len(ready) + len(after) :]
        own, outs, refs = refs[0], refs[1:PLANE], refs[PLANE:]
        kept, ring, sems, more_sems = refs[-4:]
        incoming = [
            copies(integral_ref, start + k * unit, unit, ring.at[k % SLOTS], sems.at[k % SLOTS]) for k in range(steps)
        ]
        handed = [
            copies(integral_ref, start + stream + k * unit, unit, refs[0].at[:, pl.ds(k * unit, unit)], more_sems.at[k])
            for k in range(more // unit)
        ]
        ahead = min(SLOTS - 1, steps)
        for move in incoming[0]:
            move.start()

        def tiles(chunk_ref, part, offset, sums):
            for at in range(0, unit, tile):
                for place, values in multiply(window_ref, chunk_ref, at, tile, sums):
                    columns_at = pl.ds(offset + at + place, values.shape[1])
                    for r in range(PLANE):
                        target = own if r == 0 else kept.at[r - 1]
                        for begin, rows, where in packed_rows(group, r, part):
                            target[where : where + rows, columns_at] = values[begin : begin + rows]

        def looped(sums):
            for move in sum(incoming[1:], []):
                move.start()

            @pl.loop(0, len(held))
            def _(k):
                at = pl.multiple_of(k * unit, unit)
                tiles(chunks[0].at[:, pl.ds(at, unit)], 0, at, sums)

            part, offset = divmod(len(held) * unit, width)

            @pl.loop(0, steps)
            def _(k):
                at = pl.multiple_of(k * unit, unit)
                for move in copies(integral_ref, start + at, unit, ring.at[k], sems.at[k]):
                    move.wait()
                tiles(ring.at[k], part, offset + at, sums)

        def work(*sums):
            sets = [sums[:2], sums[2:]]
            if len(chunks) == 1 and steps < SLOTS and not handed and (parts == 1 or len(held) == steps):
                return looped(sets[0])
            lead = 2
            for k in range(lead):
                tiles(held[k], *divmod(k * unit, width), sets[k % 2])
                for move in incoming[k + 1] if k + 1 < ahead else []:
                    move.start()
            for k in range(max(len(held) - lead, steps)):
                if k < steps:
                    for move in incoming[k]:
                        move.wait()
                    for move in incoming[k + SLOTS - 1] if k + SLOTS - 1 < steps else []:
                        move.start()
                    tiles(ring.at[k % SLOTS], *divmod((len(held) + k) * unit, width), sets[0])
                if k + lead < len(held):
                    tiles(held[k + lead], *divmod((k + lead) * unit, width), sets[1])
                if k % 2 == 1 and k // 2 < len(handed):
                    for move in handed[k // 2]:
                        move.start()

        held = [
            chunk_ref.at[:, pl.ds(at, unit)] for chunk_ref in chunks for at in range(0, chunk_ref.shape[1], unit)
        ]
        rows = PLANE * group
        if tile == 2 * MATRIX and depth % MATRIX == 0 and rows % 16 == 0:
            pl.run_scoped(work, *[pltpu.ACC(i % 2)((rows, MATRIX), F32) for i in range(4)])
        else:
            work()

        largest = jnp.max(jnp.abs(kept[...]), axis=(0, 1, 2), keepdims=True)[0]
        for r, out in enumerate(outs):
            code, scale = encode(kept[r], largest)
            out[:, pl.ds(0, width)] = code
            out[:, pl.ds(width, LANES)] = jnp.broadcast_to(scale, (parts * group, LANES))
        for move in sum(handed, []):
            move.wait()

    shapes = [pltpu.VMEM((parts * group, width), F32)]
    shapes += [pltpu.VMEM((parts * group, width + LANES), BF16)] * (PLANE - 1)
    if more:
        shapes.append(pltpu.VMEM((depth, more), BF16))
    ready = [pltpu.with_memory_space_constraint(chunk, pltpu.VMEM) for chunk in ready]
    return pl.pallas_call(
        kernel,
        out_shape=shapes,
        in_specs=[pl.BlockSpec(memory_space=pltpu.VMEM), pl.BlockSpec(memory_space=pl.ANY)]
        + [pl.BlockSpec(memory_space=pltpu.VMEM)] * len(ready)
        + [pl.BlockSpec(memory_space=pl.ANY)] * len(after),
        out_specs=[pl.BlockSpec(memory_space=pltpu.VMEM)] * len(shapes),
        scratch_shapes=[
            pltpu.VMEM((PLANE - 1, parts * group, width), F32),
            pltpu.VMEM((min(SLOTS, steps), depth, unit), BF16),
            pltpu.SemaphoreType.DMA((min(SLOTS, steps), PIECES)),
            pltpu.SemaphoreType.DMA((max(more // unit, 1), PIECES)),
        ],
        compiler_params=pltpu.CompilerParams(vmem_limit_bytes=VMEM),
        cost_estimate=pl.CostEstimate(
            flops=2 * window.shape[0] * depth * columns, bytes_accessed=depth * columns * 2, transcendentals=0
        ),
    )(window, integral, *ready, *after)


def add_codes(chunk):
    rows, width = chunk[0].shape

    def kernel(own_ref, *refs):
        total = own_ref[...]
        for ref in refs[:-1]:
            total += decode(ref[:, pl.ds(0, width)], ref[:, pl.ds(width, 1)])
        refs[-1][...] = total

    return pl.pallas_call(
        kernel,
        out_shape=jax.ShapeDtypeStruct((rows, width), F32),
        in_specs=[pl.BlockSpec(memory_space=pltpu.VMEM)] * len(chunk),
        out_specs=pl.BlockSpec(memory_space=pltpu.VMEM),
        compiler_params=pltpu.CompilerParams(vmem_limit_bytes=VMEM),
        cost_estimate=SMALL,
    )(*chunk)


def line_fold(widths, parts):
    return next(n for n in (8, 4, 2, 1) if n * parts <= 8 and all(width % (n * LANES) == 0 for width in widths))


def add_plane(chunks, lines, pairs):
    group = lines * pairs
    parts = fold(group)
    widths = [own.shape[1] for own, *_ in chunks]
    pieces = line_fold(widths, parts)
    rows, columns = parts * pieces * pairs, sum(widths) // pieces

    def kernel(*refs):
        ins, own, outs, kept = list(refs[: -lines - 1]), refs[-lines - 1], refs[-lines:-1], refs[-1]
        start, largest = 0, jnp.zeros((1, 1), F32)
        for i, width in enumerate(widths):
            total = ins.pop(0)[...]
            for _ in chunks[i][1:]:
                ref = ins.pop(0)
                total += decode(ref[:, pl.ds(0, width)], ref[:, pl.ds(width, 1)])
            largest = jnp.maximum(largest, jnp.max(jnp.abs(total), keepdims=True))
            piece = width // pieces
            for s in range(lines):
                for j, part in enumerate(unpacked(total, group, s * pairs, pairs)):
                    for k in range(pieces):
                        row = pl.ds((j * pieces + k) * pairs, pairs)
                        value = part[:, k * piece : (k + 1) * piece]
                        if s == 0:
                            own[row, pl.ds(start, piece)] = value
                        else:
                            kept[s - 1, row, pl.ds(start, piece)] = value
            start += piece
        for s, out in enumerate(outs):
            code, scale = encode(kept[s], largest)
            out[:, pl.ds(0, columns)] = code
            out[:, pl.ds(columns, LANES)] = jnp.broadcast_to(scale, (rows, LANES))

    code = jax.ShapeDtypeStruct((rows, columns + LANES), BF16)
    return pl.pallas_call(
        kernel,
        out_shape=[jax.ShapeDtypeStruct((rows, columns), F32)] + [code] * (lines - 1),
        in_specs=[pl.BlockSpec(memory_space=pltpu.VMEM)] * sum(map(len, chunks)),
        out_specs=[pl.BlockSpec(memory_space=pltpu.VMEM)] * lines,
        scratch_shapes=[pltpu.VMEM((lines - 1, rows, columns), F32)],
        compiler_params=pltpu.CompilerParams(vmem_limit_bytes=VMEM),
        cost_estimate=SMALL,
    )(*[ref for chunk in chunks for ref in chunk])


def add_line(own, codes, widths, parts, pairs):
    rows, columns = own.shape
    pieces = line_fold(widths, parts)

    def kernel(own_ref, *refs):
        total = own_ref[...]
        for ref in refs[:-1]:
            total += decode(ref[:, pl.ds(0, columns)], ref[:, pl.ds(columns, 1)])
        at, start = 0, 0
        for width in widths:
            piece = width // pieces
            for j in range(parts * pieces):
                refs[-1][:, pl.ds(start, piece)] = total[j * pairs : (j + 1) * pairs, at : at + piece]
                start += piece
            at += piece

    return pl.pallas_call(
        kernel,
        out_shape=jax.ShapeDtypeStruct((pairs, sum(widths) * parts), F32),
        in_specs=[pl.BlockSpec(memory_space=pltpu.VMEM)] * (1 + len(codes)),
        out_specs=pl.BlockSpec(memory_space=pltpu.VMEM),
        compiler_params=pltpu.CompilerParams(vmem_limit_bytes=VMEM),
        cost_estimate=SMALL,
    )(own, *codes)


def per_device(owners, cores, amplitudes, integral):
    pairs = amplitudes.shape[0]
    lines = owners // PLANE
    def swap(axis, size, array, by):
        return lax.ppermute(array, axis, [(i, i ^ by) for i in range(size)])

    def farthest_first(exchange, arrays):
        return [exchange(array, i + 1) for i, array in enumerate(arrays)][::-1]

    plane = functools.partial(swap, "ab", owners)
    line = lambda array, by: swap("ab", owners, array, by * PLANE)
    core = functools.partial(swap, "cd", cores)

    unit = integral.shape[1] // UNITS
    early, middle, late = (count * unit for count in AHEAD)

    parts = split_by_plane(amplitudes, lines)
    ready = [load(0, early, unit, integral, parts[0])]
    parts = [parts[0]] + farthest_first(plane, parts[1:])
    parts = split_by_line(parts, lines, pairs, ready[-1])
    ready.append(load(early, middle, unit, integral, parts[0]))
    parts = [parts[0]] + farthest_first(line, parts[1:])
    half = gather_half(parts, pairs, ready[-1])
    ready.append(load(early + middle, late, unit, integral, half))
    window = join([half] + [core(half, j) for j in range(1, cores)], ready[-1])

    start, more = early + middle + late, MORE * unit
    own, *codes, chunk = product(window, integral, ready, start, STREAM * unit, more, unit, [])
    chunks = [[own] + farthest_first(plane, codes)]
    start += STREAM * unit + more
    own, *codes = product(window, integral, [chunk], start, SECOND * unit - more, 0, unit, [own])
    chunks.append([own] + farthest_first(plane, codes))
    chunks[0] = [add_codes(chunks[0])]
    own, *codes = add_plane(chunks, lines, pairs)
    codes = farthest_first(line, codes)
    return add_line(own, codes, [chunk[0].shape[1] for chunk in chunks], fold(lines * pairs), pairs)


def solution(mesh):
    placed = (P("ab", None, "cd"), P("ab", "cd"))
    return jax.shard_map(
        functools.partial(per_device, mesh.shape["ab"], mesh.shape["cd"]),
        mesh=mesh,
        in_specs=placed,
        out_specs=P("ab", "cd"),
        check_vma=False,
    )
```

```python
import functools
import math

import jax
import jax.numpy as jnp
from jax import lax
from jax.experimental import pallas as pl
from jax.experimental.pallas import tpu as pltpu
from jax.sharding import PartitionSpec as P

F32, BF16 = jnp.float32, jnp.bfloat16
PLANE = 4
UNITS = 20
AHEAD = (2, 4, 1)
STREAM = 7
SECOND = 6
MORE = 3
SLOTS = 4
PIECES = 2
TILE = 512
MATRIX = 256
LANES = 128
TOP, TINY = 1440.0, 1e-30
SMALL = pl.CostEstimate(flops=1 << 20, bytes_accessed=1 << 20, transcendentals=0)
VMEM = 14 << 20


def select(rows, columns, source):
    row = lax.broadcasted_iota(jnp.int32, (rows, columns), 0)
    column = lax.broadcasted_iota(jnp.int32, (rows, columns), 1)
    return (column == source(row)).astype(BF16)


def copies(integral, start, unit, target, sems):
    step = target.shape[0] // PIECES
    return [
        pltpu.make_async_copy(
            integral.at[pl.ds(i * step, step), pl.ds(start, unit)],
            target.at[pl.ds(i * step, step), :],
            sems.at[i],
        )
        for i in range(PIECES)
    ]


def load(start, columns, unit, integral, after):
    depth = integral.shape[0]

    def kernel(integral_ref, after_ref, out_ref, sems):
        moves = []
        for k in range(columns // unit):
            target = out_ref.at[:, pl.ds(k * unit, unit)]
            moves += copies(integral_ref, start + k * unit, unit, target, sems.at[k])
        for move in moves:
            move.start()
        for move in moves:
            move.wait()

    return pl.pallas_call(
        kernel,
        out_shape=pltpu.VMEM((depth, columns), BF16),
        in_specs=[pl.BlockSpec(memory_space=pl.ANY)] * 2,
        out_specs=pl.BlockSpec(memory_space=pltpu.VMEM),
        scratch_shapes=[pltpu.SemaphoreType.DMA((columns // unit, PIECES))],
        compiler_params=pltpu.CompilerParams(vmem_limit_bytes=VMEM),
        cost_estimate=pl.CostEstimate(flops=0, bytes_accessed=depth * columns * 2, transcendentals=0),
    )(integral, after)


def encode(sums, largest):
    scale = (TOP / jnp.maximum(largest, TINY)).astype(BF16)
    scaled = sums * scale.astype(F32)
    square = scaled * scaled
    fourth = square * square
    return (fourth * fourth * square * (scaled * jnp.abs(scaled))).astype(BF16), scale


def decode(code, scale):
    code = code.astype(F32)
    size = jnp.exp2(jnp.log2(jnp.abs(code)) * (1.0 / 12.0)) * (1.0 / scale.astype(F32))
    return jnp.where(code < 0, -size, size)


def fold(group):
    return 8 // math.gcd(group, 8)


def window_row(row, group):
    whole = group // 8 * 8
    rest = group - whole
    if not rest:
        return row // group, row % group
    if not whole:
        return row // rest, row % rest
    behind = row - PLANE * whole
    tiled = behind < 0
    return jnp.where(tiled, row // whole, behind // rest), jnp.where(tiled, row % whole, whole + behind % rest)


def packed_rows(group, chip, part):
    whole = group // 8 * 8
    rest = group - whole
    rows = [(chip * whole, whole, part * whole)] if whole else []
    return rows + ([(PLANE * whole + chip * rest, rest, fold(group) * whole + part * rest)] if rest else [])


def unpacked(array, group, start, count):
    parts = fold(group)
    whole = group // 8 * 8
    rest = group - whole
    out = []
    for j in range(parts):
        pieces = []
        if start < whole:
            pieces.append(array[j * whole + start : j * whole + min(start + count, whole)])
        if start + count > whole:
            at = parts * whole + j * rest - whole
            pieces.append(array[at + max(start, whole) : at + start + count])
        out.append(pieces[0] if len(pieces) == 1 else jnp.concatenate(pieces, axis=0))
    return out


def split_by_plane(amplitudes, lines):
    pairs, blocks, offsets = amplitudes.shape
    group = lines * pairs

    def kernel(in_ref, *outs):
        me = lax.axis_index("ab")
        flat = in_ref[...].reshape(pairs * blocks, offsets)
        for r, out in enumerate(outs):

            def source(row):
                s, p = row // pairs, row % pairs
                return p * blocks + jnp.bitwise_xor(s * PLANE + r, me)

            taken = select(group, pairs * blocks, source)
            out[...] = jnp.dot(taken, flat, preferred_element_type=F32).astype(BF16)

    shape = jax.ShapeDtypeStruct((group, offsets), BF16)
    return pl.pallas_call(
        kernel,
        out_shape=[shape] * PLANE,
        in_specs=[pl.BlockSpec(memory_space=pltpu.VMEM)],
        out_specs=[pl.BlockSpec(memory_space=pltpu.VMEM)] * PLANE,
        compiler_params=pltpu.CompilerParams(vmem_limit_bytes=VMEM),
        cost_estimate=SMALL,
    )(amplitudes)


def split_by_line(parts, lines, pairs, after):
    group, offsets = parts[0].shape
    rows = PLANE * pairs

    def kernel(*refs):
        ins, outs = refs[:PLANE], refs[PLANE + 1 :]
        for s, out in enumerate(outs):
            total = 0.0
            for i, ref in enumerate(ins):
                r = (PLANE - i) % PLANE

                def source(row):
                    return jnp.where(row // pairs == r, s * pairs + row % pairs, -1)

                total += jnp.dot(select(rows, group, source), ref[...], preferred_element_type=F32)
            out[...] = total.astype(BF16)

    shape = jax.ShapeDtypeStruct((rows, offsets), BF16)
    return pl.pallas_call(
        kernel,
        out_shape=[shape] * lines,
        in_specs=[pl.BlockSpec(memory_space=pltpu.VMEM)] * PLANE + [pl.BlockSpec(memory_space=pl.ANY)],
        out_specs=[pl.BlockSpec(memory_space=pltpu.VMEM)] * lines,
        compiler_params=pltpu.CompilerParams(vmem_limit_bytes=VMEM),
        cost_estimate=SMALL,
    )(*parts, after)


def gather_half(parts, pairs, after):
    lines = len(parts)
    rows, offsets = parts[0].shape
    group = lines * pairs

    def kernel(*refs):
        total = 0.0
        for i in range(lines):
            s = (lines - i) % lines

            def source(row):
                r, at = window_row(row, group)
                return jnp.where(at // pairs == s, r * pairs + at % pairs, -1)

            total += jnp.dot(select(PLANE * group, rows, source), refs[i][...], preferred_element_type=F32)
        refs[-1][...] = total.astype(BF16)

    return pl.pallas_call(
        kernel,
        out_shape=jax.ShapeDtypeStruct((PLANE * group, offsets), BF16),
        in_specs=[pl.BlockSpec(memory_space=pltpu.VMEM)] * lines + [pl.BlockSpec(memory_space=pl.ANY)],
        out_specs=pl.BlockSpec(memory_space=pltpu.VMEM),
        compiler_params=pltpu.CompilerParams(vmem_limit_bytes=VMEM),
        cost_estimate=SMALL,
    )(*parts, after)


def join(halves, after):
    cores = len(halves)
    rows, offsets = halves[0].shape

    def kernel(*refs):
        core = lax.axis_index("cd")
        for c in range(cores):

            @pl.when(core == c)
            def _():
                for j in range(cores):
                    refs[-1][:, pl.ds((c ^ j) * offsets, offsets)] = refs[j][...]

    return pl.pallas_call(
        kernel,
        out_shape=jax.ShapeDtypeStruct((rows, cores * offsets), BF16),
        in_specs=[pl.BlockSpec(memory_space=pltpu.VMEM)] * cores + [pl.BlockSpec(memory_space=pl.ANY)],
        out_specs=pl.BlockSpec(memory_space=pltpu.VMEM),
        compiler_params=pltpu.CompilerParams(vmem_limit_bytes=VMEM),
        cost_estimate=SMALL,
    )(*halves, after)


def multiply(window_ref, chunk_ref, at, tile, sums):
    depth = window_ref.shape[1]
    if not sums:
        return [(0, jnp.dot(window_ref[...], chunk_ref[:, pl.ds(at, tile)], preferred_element_type=F32))]
    for k in range(depth // MATRIX):
        ks = pl.ds(k * MATRIX, MATRIX)
        for unit in range(2):
            pltpu.matmul_push_rhs(chunk_ref[ks, pl.ds(at + unit * MATRIX, MATRIX)], k % 2, unit)
        for unit in range(2):
            pltpu.matmul_acc_lhs(sums[unit], window_ref[:, ks], k % 2)
    return [(unit * MATRIX, pltpu.matmul_pop(sums[unit])) for unit in range(2)]


def product(window, integral, ready, start, stream, more, unit, after):
    group = window.shape[0] // PLANE
    depth = integral.shape[0]
    parts = fold(group)
    columns = sum(chunk.shape[1] for chunk in ready) + stream
    width = columns // parts
    tile = next(t for t in (TILE, 256, 128) if unit % t == 0)
    steps = stream // unit

    def kernel(window_ref, integral_ref, *refs):
        chunks, refs = refs[: len(ready)], refs[len(ready) + len(after) :]
        own, outs, refs = refs[0], refs[1:PLANE], refs[PLANE:]
        kept, ring, sems, more_sems = refs[-4:]
        incoming = [
            copies(integral_ref, start + k * unit, unit, ring.at[k % SLOTS], sems.at[k % SLOTS]) for k in range(steps)
        ]
        handed = [
            copies(integral_ref, start + stream + k * unit, unit, refs[0].at[:, pl.ds(k * unit, unit)], more_sems.at[k])
            for k in range(more // unit)
        ]
        ahead = min(SLOTS - 1, steps)
        for move in incoming[0]:
            move.start()

        def tiles(chunk_ref, part, offset, sums):
            for at in range(0, unit, tile):
                for place, values in multiply(window_ref, chunk_ref, at, tile, sums):
                    columns_at = pl.ds(offset + at + place, values.shape[1])
                    for r in range(PLANE):
                        target = own if r == 0 else kept.at[r - 1]
                        for begin, rows, where in packed_rows(group, r, part):
                            target[where : where + rows, columns_at] = values[begin : begin + rows]

        def looped(sums):
            for move in sum(incoming[1:], []):
                move.start()

            @pl.loop(0, len(held))
            def _(k):
                at = pl.multiple_of(k * unit, unit)
                tiles(chunks[0].at[:, pl.ds(at, unit)], 0, at, sums)

            part, offset = divmod(len(held) * unit, width)

            @pl.loop(0, steps)
            def _(k):
                at = pl.multiple_of(k * unit, unit)
                for move in copies(integral_ref, start + at, unit, ring.at[k], sems.at[k]):
                    move.wait()
                tiles(ring.at[k], part, offset + at, sums)

        def work(*sums):
            sets = [sums[:2], sums[2:]]
            if len(chunks) == 1 and steps < SLOTS and not handed and (parts == 1 or len(held) == steps):
                return looped(sets[0])
            lead = 2
            for k in range(lead):
                tiles(held[k], *divmod(k * unit, width), sets[k % 2])
                for move in incoming[k + 1] if k + 1 < ahead else []:
                    move.start()
            for k in range(max(len(held) - lead, steps)):
                if k < steps:
                    for move in incoming[k]:
                        move.wait()
                    for move in incoming[k + SLOTS - 1] if k + SLOTS - 1 < steps else []:
                        move.start()
                    tiles(ring.at[k % SLOTS], *divmod((len(held) + k) * unit, width), sets[0])
                if k + lead < len(held):
                    tiles(held[k + lead], *divmod((k + lead) * unit, width), sets[1])
                if k % 2 == 1 and k // 2 < len(handed):
                    for move in handed[k // 2]:
                        move.start()

        held = [
            chunk_ref.at[:, pl.ds(at, unit)] for chunk_ref in chunks for at in range(0, chunk_ref.shape[1], unit)
        ]
        rows = PLANE * group
        if tile == 2 * MATRIX and depth % MATRIX == 0 and rows % 16 == 0:
            pl.run_scoped(work, *[pltpu.ACC(i % 2)((rows, MATRIX), F32) for i in range(4)])
        else:
            work()

        largest = jnp.max(jnp.abs(kept[...]), axis=(0, 1, 2), keepdims=True)[0]
        for r, out in enumerate(outs):
            code, scale = encode(kept[r], largest)
            out[:, pl.ds(0, width)] = code
            out[:, pl.ds(width, LANES)] = jnp.broadcast_to(scale, (parts * group, LANES))
        for move in sum(handed, []):
            move.wait()

    shapes = [pltpu.VMEM((parts * group, width), F32)]
    shapes += [pltpu.VMEM((parts * group, width + LANES), BF16)] * (PLANE - 1)
    if more:
        shapes.append(pltpu.VMEM((depth, more), BF16))
    ready = [pltpu.with_memory_space_constraint(chunk, pltpu.VMEM) for chunk in ready]
    return pl.pallas_call(
        kernel,
        out_shape=shapes,
        in_specs=[pl.BlockSpec(memory_space=pltpu.VMEM), pl.BlockSpec(memory_space=pl.ANY)]
        + [pl.BlockSpec(memory_space=pltpu.VMEM)] * len(ready)
        + [pl.BlockSpec(memory_space=pl.ANY)] * len(after),
        out_specs=[pl.BlockSpec(memory_space=pltpu.VMEM)] * len(shapes),
        scratch_shapes=[
            pltpu.VMEM((PLANE - 1, parts * group, width), F32),
            pltpu.VMEM((min(SLOTS, steps), depth, unit), BF16),
            pltpu.SemaphoreType.DMA((min(SLOTS, steps), PIECES)),
            pltpu.SemaphoreType.DMA((max(more // unit, 1), PIECES)),
        ],
        compiler_params=pltpu.CompilerParams(vmem_limit_bytes=VMEM),
        cost_estimate=pl.CostEstimate(
            flops=2 * window.shape[0] * depth * columns, bytes_accessed=depth * columns * 2, transcendentals=0
        ),
    )(window, integral, *ready, *after)


def add_codes(chunk):
    rows, width = chunk[0].shape

    def kernel(own_ref, *refs):
        total = own_ref[...]
        for ref in refs[:-1]:
            total += decode(ref[:, pl.ds(0, width)], ref[:, pl.ds(width, 1)])
        refs[-1][...] = total

    return pl.pallas_call(
        kernel,
        out_shape=jax.ShapeDtypeStruct((rows, width), F32),
        in_specs=[pl.BlockSpec(memory_space=pltpu.VMEM)] * len(chunk),
        out_specs=pl.BlockSpec(memory_space=pltpu.VMEM),
        compiler_params=pltpu.CompilerParams(vmem_limit_bytes=VMEM),
        cost_estimate=SMALL,
    )(*chunk)


def line_fold(widths, parts):
    return next(n for n in (8, 4, 2, 1) if n * parts <= 8 and all(width % (n * LANES) == 0 for width in widths))


def add_plane(chunks, lines, pairs):
    group = lines * pairs
    parts = fold(group)
    widths = [own.shape[1] for own, *_ in chunks]
    pieces = line_fold(widths, parts)
    rows, columns = parts * pieces * pairs, sum(widths) // pieces

    def kernel(*refs):
        ins, own, outs, kept = list(refs[: -lines - 1]), refs[-lines - 1], refs[-lines:-1], refs[-1]
        start, largest = 0, jnp.zeros((1, 1), F32)
        for i, width in enumerate(widths):
            total = ins.pop(0)[...]
            for _ in chunks[i][1:]:
                ref = ins.pop(0)
                total += decode(ref[:, pl.ds(0, width)], ref[:, pl.ds(width, 1)])
            largest = jnp.maximum(largest, jnp.max(jnp.abs(total), keepdims=True))
            piece = width // pieces
            for s in range(lines):
                for j, part in enumerate(unpacked(total, group, s * pairs, pairs)):
                    for k in range(pieces):
                        row = pl.ds((j * pieces + k) * pairs, pairs)
                        value = part[:, k * piece : (k + 1) * piece]
                        if s == 0:
                            own[row, pl.ds(start, piece)] = value
                        else:
                            kept[s - 1, row, pl.ds(start, piece)] = value
            start += piece
        for s, out in enumerate(outs):
            code, scale = encode(kept[s], largest)
            out[:, pl.ds(0, columns)] = code
            out[:, pl.ds(columns, LANES)] = jnp.broadcast_to(scale, (rows, LANES))

    code = jax.ShapeDtypeStruct((rows, columns + LANES), BF16)
    return pl.pallas_call(
        kernel,
        out_shape=[jax.ShapeDtypeStruct((rows, columns), F32)] + [code] * (lines - 1),
        in_specs=[pl.BlockSpec(memory_space=pltpu.VMEM)] * sum(map(len, chunks)),
        out_specs=[pl.BlockSpec(memory_space=pltpu.VMEM)] * lines,
        scratch_shapes=[pltpu.VMEM((lines - 1, rows, columns), F32)],
        compiler_params=pltpu.CompilerParams(vmem_limit_bytes=VMEM),
        cost_estimate=SMALL,
    )(*[ref for chunk in chunks for ref in chunk])


def add_line(own, codes, widths, parts, pairs):
    rows, columns = own.shape
    pieces = line_fold(widths, parts)

    def kernel(own_ref, *refs):
        total = own_ref[...]
        for ref in refs[:-1]:
            total += decode(ref[:, pl.ds(0, columns)], ref[:, pl.ds(columns, 1)])
        at, start = 0, 0
        for width in widths:
            piece = width // pieces
            for j in range(parts * pieces):
                refs[-1][:, pl.ds(start, piece)] = total[j * pairs : (j + 1) * pairs, at : at + piece]
                start += piece
            at += piece

    return pl.pallas_call(
        kernel,
        out_shape=jax.ShapeDtypeStruct((pairs, sum(widths) * parts), F32),
        in_specs=[pl.BlockSpec(memory_space=pltpu.VMEM)] * (1 + len(codes)),
        out_specs=pl.BlockSpec(memory_space=pltpu.VMEM),
        compiler_params=pltpu.CompilerParams(vmem_limit_bytes=VMEM),
        cost_estimate=SMALL,
    )(own, *codes)


def per_device(owners, cores, amplitudes, integral):
    pairs = amplitudes.shape[0]
    lines = owners // PLANE
    def swap(axis, size, array, by):
        return lax.ppermute(array, axis, [(i, i ^ by) for i in range(size)])

    def farthest_first(exchange, arrays):
        return [exchange(array, i + 1) for i, array in enumerate(arrays)][::-1]

    plane = functools.partial(swap, "ab", owners)
    line = lambda array, by: swap("ab", owners, array, by * PLANE)
    core = functools.partial(swap, "cd", cores)

    unit = integral.shape[1] // UNITS
    early, middle, late = (count * unit for count in AHEAD)

    parts = split_by_plane(amplitudes, lines)
    ready = [load(0, early, unit, integral, parts[0])]
    parts = [parts[0]] + farthest_first(plane, parts[1:])
    parts = split_by_line(parts, lines, pairs, ready[-1])
    ready.append(load(early, middle, unit, integral, parts[0]))
    parts = [parts[0]] + farthest_first(line, parts[1:])
    half = gather_half(parts, pairs, ready[-1])
    ready.append(load(early + middle, late, unit, integral, half))
    window = join([half] + [core(half, j) for j in range(1, cores)], ready[-1])

    start, more = early + middle + late, MORE * unit
    own, *codes, chunk = product(window, integral, ready, start, STREAM * unit, more, unit, [])
    chunks = [[own] + farthest_first(plane, codes)]
    start += STREAM * unit + more
    own, *codes = product(window, integral, [chunk], start, SECOND * unit - more, 0, unit, [own])
    chunks.append([own] + farthest_first(plane, codes))
    chunks[0] = [add_codes(chunks[0])]
    own, *codes = add_plane(chunks, lines, pairs)
    codes = farthest_first(line, codes)
    return add_line(own, codes, [chunk[0].shape[1] for chunk in chunks], fold(lines * pairs), pairs)


def solution(mesh):
    placed = (P("ab", None, "cd"), P("ab", "cd"))
    return jax.shard_map(
        functools.partial(per_device, mesh.shape["ab"], mesh.shape["cd"]),
        mesh=mesh,
        in_specs=placed,
        out_specs=P("ab", "cd"),
        check_vma=False,
    )
```
